32 devices in a mesh: slide: 4 (over z), strip: 8 (over y, x, core).
Axes of the slice: x: 2, y: 2, z: 4, core: 2. Of those that a mesh axis runs over, the one named last changes fastest.
Arguments:
- image: bfloat16 [4, 48, 16, 256], P('slide', 'strip'), may hold values from -6 to 6
- cotangent: bfloat16 [4, 48, 16, 256], P('slide', 'strip'), may hold values from -6 to 6
- kernel_tall: bfloat16 [51, 5, 256], replicated, may hold values from -0.375 to 0.375
- kernel_wide: bfloat16 [5, 51, 256], replicated, may hold values from -0.375 to 0.375
- layer_norm_gain: float32 [256], replicated, may hold values from 0.5 to 1.5
- layer_norm_bias: float32 [256], replicated, may hold values from -3 to 3
- w_in: bfloat16 [256, 1024], replicated, may hold values from -0.375 to 0.375
- b_in: float32 [1024], replicated, may hold values from -3 to 3
- w_out: bfloat16 [1024, 256], replicated, may hold values from -0.1875 to 0.1875
- b_out: float32 [256], replicated, may hold values from -3 to 3
Outputs:
- output: bfloat16 [4, 48, 16, 256], P('slide', 'strip')
- grad_image: bfloat16 [4, 48, 16, 256], P('slide', 'strip')
- grad_tall: float32 [51, 5, 256], replicated
- grad_wide: float32 [5, 51, 256], replicated
- grad_gain: float32 [256], replicated
- grad_shift: float32 [256], replicated
- grad_w_in: float32 [256, 1024], replicated
- grad_b_in: float32 [1024], replicated
- grad_w_out: float32 [1024, 256], replicated
- grad_b_out: float32 [256], replicated
The draws below stay inside these ranges and needn't reach their ends.
All inputs are finite; a program needn't handle non-finite values.
Results may differ from the reference program's by a relative error of at most 0.0085.
Values may be sent and summed in bfloat16 or wider, within the bound.
A program may use at most 64 MiB of HBM per device.

```python
import jax
import jax.numpy as jnp
from jax import lax

C = 256
FF = 1024
LONG = 51
SHORT = 5
H = 48
W = 16
SLIDES = 4
CELLS = 3072


def levels(key, dims, shards, least, largest):
    level, own = 1.0, jax.random.fold_in(key, 6)
    for dim, blocks in shards:
        draws = jnp.exp(jax.random.uniform(jax.random.fold_in(own, dim), (blocks,), jnp.float32, least / len(shards), largest / len(shards)))
        level = level * jnp.repeat(draws, dims[dim] // blocks).reshape([-1 if axis == dim else 1 for axis in range(len(dims))])
    return level


def normal_values(stream_key, extent, scale, bound, pieces=(), dtype=jnp.bfloat16):
    values = jax.random.normal(stream_key, extent, jnp.float32) * scale
    if len(pieces) > 0:
        values = levels(stream_key, extent, pieces, -0.22, 0.18) * values
    return jnp.clip(values, min=-bound, max=bound).astype(dtype)


def setup_inputs(seed: int = 0) -> dict:
    streams_of = jax.random.split(jax.random.key(seed), 11)
    image = normal_values(streams_of[0], (SLIDES, H, W, C), 1.0, 6.0, ((0, 4), (1, 8)))
    cotangent = normal_values(streams_of[1], (SLIDES, H, W, C), 1.0, 6.0, ((0, 4), (1, 8)))
    kernel_tall = normal_values(streams_of[2], (LONG, SHORT, C), (LONG * SHORT) ** -0.5, 0.375)
    kernel_wide = normal_values(streams_of[3], (SHORT, LONG, C), (LONG * SHORT) ** -0.5, 0.375)
    layer_norm_gain = jnp.clip(jax.random.uniform(streams_of[4], (C,), jnp.float32, 0.5, 1.5), 0.5, 1.5)
    layer_norm_bias = normal_values(streams_of[5], (C,), 0.5, 3.0, (), jnp.float32)
    w_in = normal_values(streams_of[6], (C, FF), C ** -0.5, 0.375)
    b_in = normal_values(streams_of[7], (FF,), 0.5, 3.0, (), jnp.float32)
    w_out = normal_values(streams_of[8], (FF, C), FF ** -0.5, 0.1875)
    b_out = normal_values(streams_of[9], (C,), 0.5, 3.0, (), jnp.float32)
    return {"image": image, "cotangent": cotangent, "kernel_tall": kernel_tall, "kernel_wide": kernel_wide, "layer_norm_gain": layer_norm_gain, "layer_norm_bias": layer_norm_bias, "w_in": w_in, "b_in": b_in, "w_out": w_out, "b_out": b_out}


epsilon = 1e-06

def depth_conv(source, kernel, pad_rows, pad_cols):
    return lax.conv_general_dilated(source[None], kernel[:, :, None, :], (1, 1), ((pad_rows, pad_rows), (pad_cols, pad_cols)), dimension_numbers=('NHWC', 'HWIO', 'NHWC'), feature_group_count=source.shape[-1], preferred_element_type=jnp.float32)[0]

def kernel_grad(padded, upstream):
    return lax.conv_general_dilated(padded[None], upstream[:, :, None, :], (1, 1), 'VALID', dimension_numbers=('NHWC', 'HWIO', 'NHWC'), feature_group_count=padded.shape[-1], preferred_element_type=jnp.float32)[0]

def one_region(image, cotangent, kernel_tall, kernel_wide, layer_norm_gain, layer_norm_bias, w_in, b_in, w_out, b_out):
    tall_pad = (kernel_tall.shape[0] - 1) // 2
    rim_width = (kernel_tall.shape[1] - 1) // 2
    wide_pad = (kernel_wide.shape[1] - 1) // 2
    channels = image.shape[-1]
    mixed = depth_conv(image, kernel_tall, tall_pad, rim_width).astype(jnp.bfloat16)
    conv_out = depth_conv(mixed, kernel_wide, rim_width, wide_pad)
    mean_removed = conv_out - lax.optimization_barrier(jnp.mean(conv_out, axis=-1, keepdims=True))
    inverse_deviation = lax.rsqrt(lax.optimization_barrier(jnp.mean(mean_removed * mean_removed, axis=-1, keepdims=True)) + epsilon)
    standardized_input = mean_removed * inverse_deviation
    normalized_output = (standardized_input * layer_norm_gain + layer_norm_bias).astype(jnp.bfloat16)
    flat_normed = normalized_output.reshape(-1, channels)
    pre_act = jnp.dot(flat_normed, w_in, preferred_element_type=jnp.float32) + b_in
    cdf_value = 0.5 * (1.0 + lax.erf(pre_act * 0.7071067811865476))
    hidden = (pre_act * cdf_value).astype(jnp.bfloat16)
    branch = jnp.dot(hidden, w_out, preferred_element_type=jnp.float32) + b_out
    output = (image.astype(jnp.float32) + branch.reshape(image.shape)).astype(jnp.bfloat16)
    flat_cot = cotangent.reshape(-1, channels)
    g_w_out = jnp.dot(hidden.T, flat_cot, preferred_element_type=jnp.float32)
    g_b_out = lax.optimization_barrier(jnp.sum(flat_cot.astype(jnp.float32), axis=0))
    d_hidden = jnp.dot(flat_cot, w_out.T, preferred_element_type=jnp.float32)
    slope = cdf_value + pre_act * jnp.exp(-0.5 * pre_act * pre_act) * 0.3989422804014327
    d_pre = (d_hidden * slope).astype(jnp.bfloat16)
    g_w_in = jnp.dot(flat_normed.T, d_pre, preferred_element_type=jnp.float32)
    g_b_in = lax.optimization_barrier(jnp.sum(lax.optimization_barrier(d_pre).astype(jnp.float32), axis=0))
    grad_layer_norm = jnp.dot(d_pre, w_in.T, preferred_element_type=jnp.float32).reshape(image.shape)
    grad_norm_gain = lax.optimization_barrier(jnp.sum(grad_layer_norm * standardized_input, axis=(0, 1)))
    g_shift = lax.optimization_barrier(jnp.sum(grad_layer_norm, axis=(0, 1)))
    grad_standardized = grad_layer_norm * layer_norm_gain
    grad_depth_output = (inverse_deviation * (grad_standardized - lax.optimization_barrier(jnp.mean(grad_standardized, axis=-1, keepdims=True)) - standardized_input * lax.optimization_barrier(jnp.mean(grad_standardized * standardized_input, axis=-1, keepdims=True)))).astype(jnp.bfloat16)
    d_mixed = depth_conv(grad_depth_output, kernel_wide[::-1, ::-1], rim_width, wide_pad).astype(jnp.bfloat16)
    g_wide = kernel_grad(jnp.pad(mixed, ((rim_width, rim_width), (wide_pad, wide_pad), (0, 0))), grad_depth_output)
    d_image = depth_conv(d_mixed, kernel_tall[::-1, ::-1], tall_pad, rim_width).astype(jnp.bfloat16)
    g_tall = kernel_grad(jnp.pad(image, ((tall_pad, tall_pad), (rim_width, rim_width), (0, 0))), d_mixed)
    grad_image = (cotangent.astype(jnp.float32) + lax.optimization_barrier(d_image).astype(jnp.float32)).astype(jnp.bfloat16)
    return (output, grad_image, (g_tall, g_wide, grad_norm_gain, g_shift, g_w_in, g_b_in, g_w_out, g_b_out))

def reference(image, cotangent, kernel_tall, kernel_wide, layer_norm_gain, layer_norm_bias, w_in, b_in, w_out, b_out):

    def per_region(pair):
        return one_region(pair[0], pair[1], kernel_tall, kernel_wide, layer_norm_gain, layer_norm_bias, w_in, b_in, w_out, b_out)
    output, grad_image, grads = lax.map(per_region, (image, cotangent))
    scale_multiplier = jnp.float32(CELLS) ** (-0.5)
    summed = [lax.optimization_barrier(jnp.sum(item, axis=0)) * scale_multiplier for item in grads]
    return (output, grad_image, summed[0], summed[1], summed[2], summed[3], summed[4], summed[5], summed[6], summed[7])
```

```python
import functools

import jax
import jax.numpy as jnp
from jax import lax
from jax.experimental import pallas as pl
from jax.experimental.pallas import tpu as pltpu
from jax.sharding import PartitionSpec as P

epsilon = 1e-06
vmem_bytes = 48 * 1024 * 1024
MESH = pl.DeviceIdType.MESH


def enter(peers):
    barrier = pltpu.get_barrier_semaphore()
    for peer in peers:
        pl.semaphore_signal(barrier, inc=1, device_id=peer, device_id_type=MESH)
    pl.semaphore_wait(barrier, len(peers))


def send(src, dst, send_sem, recv_sem, index, peer):
    copy = pltpu.make_async_remote_copy(
        src_ref=src,
        dst_ref=dst,
        send_sem=send_sem.at[index],
        recv_sem=recv_sem.at[index],
        device_id=peer,
        device_id_type=MESH,
    )
    copy.start()
    return copy


def gather_kernel(count, own_ref, all_ref, send_sem, recv_sem):
    me = lax.axis_index("strip")
    peers = [{"strip": lax.rem(me + step, count)} for step in range(1, count)]
    enter(peers)
    copies = [
        send(own_ref, all_ref.at[me], send_sem, recv_sem, index, peer)
        for index, peer in enumerate(peers)
    ]
    all_ref[me] = own_ref[...]
    for copy in copies:
        copy.wait()


def gather_rows(own, collective_id):
    count = lax.axis_size("strip")
    rows, width, channels = own.shape
    gathered = pl.pallas_call(
        functools.partial(gather_kernel, count),
        out_shape=jax.ShapeDtypeStruct((count, rows * width, channels), own.dtype),
        in_specs=[pl.BlockSpec(memory_space=pltpu.VMEM)],
        out_specs=pl.BlockSpec(memory_space=pltpu.VMEM),
        scratch_shapes=[
            pltpu.SemaphoreType.DMA((count - 1,)),
            pltpu.SemaphoreType.DMA((count - 1,)),
        ],
        compiler_params=pltpu.CompilerParams(
            collective_id=collective_id, has_side_effects=True, vmem_limit_bytes=vmem_bytes
        ),
    )(own.reshape(rows * width, channels))
    return gathered.reshape(count * rows, width, channels)


def rim_kernel(count, size, own_ref, rims_ref, send_sem, recv_sem):
    me = lax.axis_index("strip")
    after = {"strip": lax.rem(me + 1, count)}
    before = {"strip": lax.rem(me + count - 1, count)}
    total = own_ref.shape[0]
    enter([after, before])
    copies = [
        send(own_ref.at[pl.ds(total - size, size)], rims_ref.at[0], send_sem, recv_sem, 0, after),
        send(own_ref.at[pl.ds(0, size)], rims_ref.at[1], send_sem, recv_sem, 1, before),
    ]
    for copy in copies:
        copy.wait()


def add_rims(own, rim_width, collective_id):
    count = lax.axis_size("strip")
    me = lax.axis_index("strip")
    rows, width, channels = own.shape
    size = rim_width * width
    rims = pl.pallas_call(
        functools.partial(rim_kernel, count, size),
        out_shape=jax.ShapeDtypeStruct((2, size, channels), own.dtype),
        in_specs=[pl.BlockSpec(memory_space=pltpu.VMEM)],
        out_specs=pl.BlockSpec(memory_space=pltpu.VMEM),
        scratch_shapes=[pltpu.SemaphoreType.DMA((2,)), pltpu.SemaphoreType.DMA((2,))],
        compiler_params=pltpu.CompilerParams(
            collective_id=collective_id, has_side_effects=True, vmem_limit_bytes=vmem_bytes
        ),
    )(own.reshape(rows * width, channels))
    rims = rims.reshape(2, rim_width, width, channels)
    above = jnp.where(me > 0, rims[0], 0)
    below = jnp.where(me < count - 1, rims[1], 0)
    return jnp.concatenate([above, own, below], axis=0)


def sum_kernel(
    strips,
    slides,
    groups,
    w_in_ref,
    w_out_ref,
    rest_ref,
    own_ref,
    w_in_sum,
    w_out_sum,
    rest_sum,
    all_ref,
    total,
    outbox,
    inbox,
    slide_out,
    slide_in,
    joint,
    result,
    send_sem,
    recv_sem,
    own_send_sem,
    own_recv_sem,
):
    me = lax.axis_index("strip")
    slide = lax.axis_index("slide")
    channels = total.shape[1]
    bits = [1 << k for k in range(strips.bit_length() - 1)]
    orders = (bits, bits[:1] + bits[:0:-1])
    mine = {bit: lax.rem(me // bit, 2) for bit in bits}
    partner = {bit: {"strip": me + bit - 2 * bit * mine[bit]} for bit in bits}
    neighbours = [{"strip": lax.rem(me + step, strips)} for step in range(1, strips)]
    others = [{"slide": lax.rem(slide + step, slides)} for step in range(1, slides)]
    enter(neighbours + others)

    inner, ff = w_in_ref.shape
    w_rows = (ff // channels) * inner
    out_rows = w_out_ref.shape[0]
    sources = [
        (k * inner, inner, w_in_ref, w_in_sum, pl.ds(k * channels, channels))
        for k in range(ff // channels)
    ]
    sources.append((w_rows, out_rows, w_out_ref, w_out_sum, slice(None)))
    sources.append((w_rows + out_rows, rest_ref.shape[0], rest_ref, rest_sum, slice(None)))

    def segments(low, high):
        for first, length, given, summed, lanes in sources:
            start, end = max(low, first), min(high, first + length)
            if start < end:
                yield pl.ds(start, end - start), pl.ds(start - first, end - start), given, summed, lanes

    def sum_rows(low, high, index):
        for here, there, given, _, lanes in segments(low, high):
            total[here] = given[there, lanes]
        rows = high - low
        piece = rows // strips
        part = piece // slides
        size = rows // 2
        starts = [low, low + size]
        trail = []
        box = low - low // strips
        for stage in range(len(bits)):
            size //= 2
            copies = []
            for half in range(2):
                bit = orders[half][stage]
                away = pl.multiple_of(starts[half] + (1 - mine[bit]) * size, 16)
                outbox[pl.ds(box, size)] = total[pl.ds(away, size)].astype(outbox.dtype)
                copies.append(
                    send(
                        outbox.at[pl.ds(box, size)],
                        inbox.at[pl.ds(box, size)],
                        send_sem,
                        recv_sem,
                        index,
                        partner[bit],
                    )
                )
                starts[half] = starts[half] + mine[bit] * size
                box += size
                index += 1
            trail.append(size)
            yield
            for half in range(2):
                copies[half].wait()
                here = pl.ds(pl.multiple_of(starts[half], 16), size)
                total[here] += inbox[pl.ds(box - (2 - half) * size, size)].astype(jnp.float32)

        kept = [pl.ds(pl.multiple_of(starts[half], 16), size) for half in range(2)]
        base = low // strips
        for half in range(2):
            slide_out[pl.ds(base + half * size, size)] = total[kept[half]].astype(slide_out.dtype)
        copies, landed = [], []
        for step, peer in enumerate(others):
            their = pl.multiple_of(base + peer["slide"] * part, 16)
            landed.append(pl.ds(base // slides + step * (slide_in.shape[0] // (slides - 1)), part))
            copies.append(
                send(
                    slide_out.at[pl.ds(their, part)],
                    slide_in.at[landed[step]],
                    send_sem,
                    recv_sem,
                    index,
                    peer,
                )
            )
            index += 1
        yield
        own = pl.ds(pl.multiple_of(base + slide * part, 16), part)
        value = slide_out[own].astype(jnp.float32)
        for step, copy in enumerate(copies):
            copy.wait()
            value += slide_in[landed[step]].astype(jnp.float32)
        joint[own] = value.astype(joint.dtype)
        copies = []
        for peer in others:
            copies.append(send(joint.at[own], joint.at[own], send_sem, recv_sem, index, peer))
            index += 1
        yield
        for copy in copies:
            copy.wait()
        for half in range(2):
            result[kept[half]] = joint[pl.ds(base + half * size, size)]

        for stage in reversed(range(len(bits))):
            size = trail[stage]
            copies = []
            for half in range(2):
                bit = orders[half][stage]
                here = pl.ds(pl.multiple_of(starts[half], 16), size)
                copies.append(
                    send(result.at[here], result.at[here], send_sem, recv_sem, index, partner[bit])
                )
                starts[half] = starts[half] - mine[bit] * size
                index += 1
            yield
            for copy in copies:
                copy.wait()
        for here, there, _, summed, lanes in segments(low, high):
            summed[there, lanes] = result[here].astype(jnp.float32)

    each = 4 * len(bits) + 2 * (slides - 1)
    running = [sum_rows(low, high, k * each) for k, (low, high) in enumerate(groups)]
    rounds = 0
    own_copies = []
    while running:
        left = []
        for group in running:
            try:
                next(group)
                left.append(group)
            except StopIteration:
                pass
        running = left
        if rounds == len(bits):
            own_copies = [
                send(own_ref, all_ref.at[me], own_send_sem, own_recv_sem, index, peer)
                for index, peer in enumerate(neighbours)
            ]
            all_ref[me] = own_ref[...]
        rounds += 1
    for copy in own_copies:
        copy.wait()


def sum_grads(g_w_in, g_w_out, others, own):
    strips, slides = lax.axis_size("strip"), lax.axis_size("slide")
    channels = g_w_out.shape[1]
    height, width = own.shape[:2]
    flat = [other.reshape(-1, channels) for other in others]
    unit = strips * slides * 16
    w_rows = g_w_in.size // channels + g_w_out.shape[0]
    used = w_rows + sum(other.shape[0] for other in flat)
    units = -(-used // unit)
    rows = units * unit
    if rows > used:
        flat.append(jnp.zeros((rows - used, channels), jnp.float32))
    rest = jnp.concatenate(flat, axis=0)
    parts = min(units, 3)
    edges = [-(-units * k // parts) * unit for k in range(parts + 1)]
    groups = tuple(zip(edges[:-1], edges[1:]))
    stages = strips.bit_length() - 1
    count = parts * (4 * stages + 2 * (slides - 1))
    piece = rows // strips
    small = jnp.bfloat16
    w_in_sum, w_out_sum, rest_sum, region = pl.pallas_call(
        functools.partial(sum_kernel, strips, slides, groups),
        out_shape=[
            jax.ShapeDtypeStruct(g_w_in.shape, jnp.float32),
            jax.ShapeDtypeStruct(g_w_out.shape, jnp.float32),
            jax.ShapeDtypeStruct(rest.shape, jnp.float32),
            jax.ShapeDtypeStruct((strips, height * width, channels), own.dtype),
        ],
        in_specs=[pl.BlockSpec(memory_space=pltpu.VMEM)] * 4,
        out_specs=[pl.BlockSpec(memory_space=pltpu.VMEM)] * 4,
        scratch_shapes=[
            pltpu.VMEM((rows, channels), jnp.float32),
            pltpu.VMEM((rows - piece, channels), small),
            pltpu.VMEM((rows - piece, channels), small),
            pltpu.VMEM((piece, channels), small),
            pltpu.VMEM(((slides - 1) * (piece // slides), channels), small),
            pltpu.VMEM((piece, channels), small),
            pltpu.VMEM((rows, channels), small),
            pltpu.SemaphoreType.DMA((count,)),
            pltpu.SemaphoreType.DMA((count,)),
            pltpu.SemaphoreType.DMA((strips - 1,)),
            pltpu.SemaphoreType.DMA((strips - 1,)),
        ],
        compiler_params=pltpu.CompilerParams(
            collective_id=3, has_side_effects=True, vmem_limit_bytes=vmem_bytes
        ),
    )(g_w_in, g_w_out, rest, own.reshape(height * width, channels))
    summed, at = [], 0
    for other in others:
        length = other.size // channels
        summed.append(rest_sum[at : at + length].reshape(other.shape))
        at += length
    return w_in_sum, w_out_sum, summed, region.reshape(strips * height, width, channels)


def rows_around(region, margin, side, rows):
    padded = jnp.pad(region, ((margin, margin), (side, side), (0, 0)))
    start = lax.axis_index("strip") * rows
    return lax.dynamic_slice_in_dim(padded, start, rows + 2 * margin, axis=0)


def depth_conv(source, kernel, pad_rows, pad_cols):
    return lax.conv_general_dilated(
        source[None],
        kernel[:, :, None, :],
        (1, 1),
        ((pad_rows, pad_rows), (pad_cols, pad_cols)),
        dimension_numbers=("NHWC", "HWIO", "NHWC"),
        feature_group_count=source.shape[-1],
        preferred_element_type=jnp.float32,
    )[0]


def kernel_grad(padded, upstream):
    return lax.conv_general_dilated(
        padded[None],
        upstream[:, :, None, :],
        (1, 1),
        "VALID",
        dimension_numbers=("NHWC", "HWIO", "NHWC"),
        feature_group_count=padded.shape[-1],
        preferred_element_type=jnp.float32,
    )[0]


def local(
    image,
    cotangent,
    kernel_tall,
    kernel_wide,
    layer_norm_gain,
    layer_norm_bias,
    w_in,
    b_in,
    w_out,
    b_out,
):
    source = image[0]
    upstream = cotangent[0]
    row_count, full_width, channels = source.shape
    tall_pad = (kernel_tall.shape[0] - 1) // 2
    rim_width = (kernel_tall.shape[1] - 1) // 2
    wide_pad = (kernel_wide.shape[1] - 1) // 2
    scale_multiplier = jnp.float32(
        row_count * full_width * lax.axis_size("slide") * lax.axis_size("strip")
    ) ** (-0.5)
    reach = min(wide_pad, full_width - 1)
    near = kernel_wide[:, wide_pad - reach : wide_pad + reach + 1]
    region_rows = row_count * lax.axis_size("strip")
    window = rows_around(gather_rows(source, 0), tall_pad + rim_width, rim_width, row_count)
    place = (
        lax.axis_index("strip") * row_count
        - rim_width
        + lax.broadcasted_iota(jnp.int32, (row_count + 2 * rim_width, 1, 1), 0)
    )
    mixed_rows = jnp.where(
        (place >= 0) & (place < region_rows), depth_conv(window, kernel_tall, 0, 0), 0.0
    ).astype(jnp.bfloat16)
    conv_out = depth_conv(mixed_rows, near, 0, reach)
    mean_removed = conv_out - jnp.mean(conv_out, axis=-1, keepdims=True)
    inverse_deviation = lax.rsqrt(
        jnp.mean(mean_removed * mean_removed, axis=-1, keepdims=True) + epsilon
    )
    standardized_input = mean_removed * inverse_deviation
    normalized_output = (standardized_input * layer_norm_gain + layer_norm_bias).astype(
        jnp.bfloat16
    )
    flat_normed = normalized_output.reshape(-1, channels)
    pre_act = jnp.dot(flat_normed, w_in, preferred_element_type=jnp.float32) + b_in
    cdf_value = 0.5 * (1.0 + lax.erf(pre_act * 0.7071067811865476))
    hidden = (pre_act * cdf_value).astype(jnp.bfloat16)
    branch = jnp.dot(hidden, w_out, preferred_element_type=jnp.float32) + b_out
    output = (source.astype(jnp.float32) + branch.reshape(source.shape)).astype(jnp.bfloat16)
    flat_cot = upstream.reshape(-1, channels)
    g_w_out = jnp.dot(hidden.T, flat_cot, preferred_element_type=jnp.float32) * scale_multiplier
    g_b_out = jnp.sum(flat_cot.astype(jnp.float32), axis=0) * scale_multiplier
    d_hidden = jnp.dot(flat_cot, w_out.T, preferred_element_type=jnp.float32)
    slope = cdf_value + pre_act * jnp.exp(-0.5 * pre_act * pre_act) * 0.3989422804014327
    d_pre = (d_hidden * slope).astype(jnp.bfloat16)
    g_w_in = jnp.dot(flat_normed.T, d_pre, preferred_element_type=jnp.float32) * scale_multiplier
    g_b_in = jnp.sum(d_pre.astype(jnp.float32), axis=0) * scale_multiplier
    grad_layer_norm = jnp.dot(d_pre, w_in.T, preferred_element_type=jnp.float32).reshape(
        source.shape
    )
    grad_norm_gain = jnp.sum(grad_layer_norm * standardized_input, axis=(0, 1)) * scale_multiplier
    g_shift = jnp.sum(grad_layer_norm, axis=(0, 1)) * scale_multiplier
    grad_standardized = grad_layer_norm * layer_norm_gain
    grad_depth_output = (
        inverse_deviation
        * (
            grad_standardized
            - jnp.mean(grad_standardized, axis=-1, keepdims=True)
            - standardized_input
            * jnp.mean(grad_standardized * standardized_input, axis=-1, keepdims=True)
        )
    ).astype(jnp.bfloat16)
    d_conv_rims = add_rims(grad_depth_output, rim_width, 1)
    d_mixed = depth_conv(d_conv_rims, near[::-1, ::-1], 0, reach).astype(jnp.bfloat16)
    g_near = (
        kernel_grad(jnp.pad(mixed_rows, ((0, 0), (reach, reach), (0, 0))), grad_depth_output)
        * scale_multiplier
    )
    g_tall = kernel_grad(window[rim_width:-rim_width], d_mixed) * scale_multiplier
    g_w_in, g_w_out, (g_tall, g_near, grad_norm_gain, g_shift, g_b_in, g_b_out), d_region = sum_grads(
        g_w_in,
        g_w_out,
        (g_tall, g_near, grad_norm_gain, g_shift, g_b_in, g_b_out),
        d_mixed,
    )
    d_mixed_window = rows_around(d_region, tall_pad, rim_width, row_count)
    d_image = depth_conv(d_mixed_window, kernel_tall[::-1, ::-1], 0, 0).astype(jnp.bfloat16)
    grad_image = (upstream.astype(jnp.float32) + d_image.astype(jnp.float32)).astype(jnp.bfloat16)
    g_wide = jnp.pad(g_near, ((0, 0), (wide_pad - reach, wide_pad - reach), (0, 0)))
    return (
        output[None],
        grad_image[None],
        g_tall,
        g_wide,
        grad_norm_gain,
        g_shift,
        g_w_in,
        g_b_in,
        g_w_out,
        g_b_out,
    )


def solution(mesh):
    placed = (
        P("slide", "strip", None, None),
        P("slide", "strip", None, None),
        P(),
        P(),
        P(),
        P(),
        P(),
        P(),
        P(),
        P(),
    )
    return jax.shard_map(
        local,
        mesh=mesh,
        in_specs=placed,
        out_specs=(
            P("slide", "strip", None, None),
            P("slide", "strip", None, None),
            P(),
            P(),
            P(),
            P(),
            P(),
            P(),
            P(),
            P(),
        ),
        check_vma=False,
    )
```

```python
import functools
import math

import jax
import jax.numpy as jnp
from jax import lax
from jax.experimental import pallas as pl
from jax.experimental.pallas import tpu as pltpu
from jax.sharding import PartitionSpec as P

epsilon = 1e-06
MESH = pl.DeviceIdType.MESH


def vmem_for(*arrays):
    return 4 * 1024 * 1024 + sum(math.prod(shape) * width for shape, width in arrays)


def enter(peers):
    barrier = pltpu.get_barrier_semaphore()
    for peer in peers:
        pl.semaphore_signal(barrier, inc=1, device_id=peer, device_id_type=MESH)
    pl.semaphore_wait(barrier, len(peers))


def send(src, dst, send_sem, recv_sem, index, peer):
    copy = pltpu.make_async_remote_copy(
        src_ref=src,
        dst_ref=dst,
        send_sem=send_sem.at[index],
        recv_sem=recv_sem.at[index],
        device_id=peer,
        device_id_type=MESH,
    )
    copy.start()
    return copy


def gather_kernel(count, own_ref, all_ref, send_sem, recv_sem):
    me = lax.axis_index("strip")
    peers = [{"strip": lax.rem(me + step, count)} for step in range(1, count)]
    enter(peers)
    copies = [
        send(own_ref, all_ref.at[me], send_sem, recv_sem, index, peer)
        for index, peer in enumerate(peers)
    ]
    all_ref[me] = own_ref[...]
    for copy in copies:
        copy.wait()


def gather_rows(own, collective_id):
    count = lax.axis_size("strip")
    rows, width, channels = own.shape
    gathered = pl.pallas_call(
        functools.partial(gather_kernel, count),
        out_shape=jax.ShapeDtypeStruct((count, rows * width, channels), own.dtype),
        in_specs=[pl.BlockSpec(memory_space=pltpu.VMEM)],
        out_specs=pl.BlockSpec(memory_space=pltpu.VMEM),
        scratch_shapes=[
            pltpu.SemaphoreType.DMA((count - 1,)),
            pltpu.SemaphoreType.DMA((count - 1,)),
        ],
        compiler_params=pltpu.CompilerParams(
            collective_id=collective_id,
            has_side_effects=True,
            vmem_limit_bytes=vmem_for((own.shape, 2), ((count, *own.shape), 2)),
        ),
    )(own.reshape(rows * width, channels))
    return gathered.reshape(count * rows, width, channels)


def rim_kernel(count, size, own_ref, rims_ref, send_sem, recv_sem):
    me = lax.axis_index("strip")
    after = {"strip": lax.rem(me + 1, count)}
    before = {"strip": lax.rem(me + count - 1, count)}
    total = own_ref.shape[0]
    enter([after, before])
    copies = [
        send(own_ref.at[pl.ds(total - size, size)], rims_ref.at[0], send_sem, recv_sem, 0, after),
        send(own_ref.at[pl.ds(0, size)], rims_ref.at[1], send_sem, recv_sem, 1, before),
    ]
    for copy in copies:
        copy.wait()


def add_rims(own, rim_width, collective_id):
    count = lax.axis_size("strip")
    me = lax.axis_index("strip")
    rows, width, channels = own.shape
    size = rim_width * width
    rims = pl.pallas_call(
        functools.partial(rim_kernel, count, size),
        out_shape=jax.ShapeDtypeStruct((2, size, channels), own.dtype),
        in_specs=[pl.BlockSpec(memory_space=pltpu.VMEM)],
        out_specs=pl.BlockSpec(memory_space=pltpu.VMEM),
        scratch_shapes=[pltpu.SemaphoreType.DMA((2,)), pltpu.SemaphoreType.DMA((2,))],
        compiler_params=pltpu.CompilerParams(
            collective_id=collective_id,
            has_side_effects=True,
            vmem_limit_bytes=vmem_for((own.shape, 2), ((2, size, channels), 2)),
        ),
    )(own.reshape(rows * width, channels))
    rims = rims.reshape(2, rim_width, width, channels)
    above = jnp.where(me > 0, rims[0], 0)
    below = jnp.where(me < count - 1, rims[1], 0)
    return jnp.concatenate([above, own, below], axis=0)


def sum_kernel(
    strips,
    slides,
    groups,
    w_in_ref,
    w_out_ref,
    rest_ref,
    own_ref,
    w_in_sum,
    w_out_sum,
    rest_sum,
    all_ref,
    total,
    outbox,
    inbox,
    slide_out,
    slide_in,
    joint,
    result,
    send_sem,
    recv_sem,
    own_send_sem,
    own_recv_sem,
):
    me = lax.axis_index("strip")
    slide = lax.axis_index("slide")
    channels = total.shape[1]
    bits = [1 << k for k in range(strips.bit_length() - 1)]
    orders = (bits, bits[:1] + bits[:0:-1])
    mine = {bit: lax.rem(me // bit, 2) for bit in bits}
    partner = {bit: {"strip": me + bit - 2 * bit * mine[bit]} for bit in bits}
    neighbours = [{"strip": lax.rem(me + step, strips)} for step in range(1, strips)]
    others = [{"slide": lax.rem(slide + step, slides)} for step in range(1, slides)]
    enter(neighbours + others)

    inner, ff = w_in_ref.shape
    w_rows = (ff // channels) * inner
    out_rows = w_out_ref.shape[0]
    sources = [
        (k * inner, inner, w_in_ref, w_in_sum, pl.ds(k * channels, channels))
        for k in range(ff // channels)
    ]
    sources.append((w_rows, out_rows, w_out_ref, w_out_sum, slice(None)))
    sources.append((w_rows + out_rows, rest_ref.shape[0], rest_ref, rest_sum, slice(None)))

    def segments(low, high):
        for first, length, given, summed, lanes in sources:
            start, end = max(low, first), min(high, first + length)
            if start < end:
                yield pl.ds(start, end - start), pl.ds(start - first, end - start), given, summed, lanes

    def sum_rows(low, high, index):
        for here, there, given, _, lanes in segments(low, high):
            total[here] = given[there, lanes]
        rows = high - low
        piece = rows // strips
        part = piece // slides
        size = rows // 2
        starts = [low, low + size]
        trail = []
        box = low - low // strips
        for stage in range(len(bits)):
            size //= 2
            copies = []
            for half in range(2):
                bit = orders[half][stage]
                away = pl.multiple_of(starts[half] + (1 - mine[bit]) * size, 16)
                outbox[pl.ds(box, size)] = total[pl.ds(away, size)].astype(outbox.dtype)
                copies.append(
                    send(
                        outbox.at[pl.ds(box, size)],
                        inbox.at[pl.ds(box, size)],
                        send_sem,
                        recv_sem,
                        index,
                        partner[bit],
                    )
                )
                starts[half] = starts[half] + mine[bit] * size
                box += size
                index += 1
            trail.append(size)
            yield
            for half in range(2):
                copies[half].wait()
                here = pl.ds(pl.multiple_of(starts[half], 16), size)
                total[here] += inbox[pl.ds(box - (2 - half) * size, size)].astype(jnp.float32)

        kept = [pl.ds(pl.multiple_of(starts[half], 16), size) for half in range(2)]
        base = low // strips
        for half in range(2):
            slide_out[pl.ds(base + half * size, size)] = total[kept[half]].astype(slide_out.dtype)
        copies, landed = [], []
        for step, peer in enumerate(others):
            their = pl.multiple_of(base + peer["slide"] * part, 16)
            landed.append(pl.ds(base // slides + step * (slide_in.shape[0] // (slides - 1)), part))
            copies.append(
                send(
                    slide_out.at[pl.ds(their, part)],
                    slide_in.at[landed[step]],
                    send_sem,
                    recv_sem,
                    index,
                    peer,
                )
            )
            index += 1
        yield
        own = pl.ds(pl.multiple_of(base + slide * part, 16), part)
        value = slide_out[own].astype(jnp.float32)
        for step, copy in enumerate(copies):
            copy.wait()
            value += slide_in[landed[step]].astype(jnp.float32)
        joint[own] = value.astype(joint.dtype)
        copies = []
        for peer in others:
            copies.append(send(joint.at[own], joint.at[own], send_sem, recv_sem, index, peer))
            index += 1
        yield
        for copy in copies:
            copy.wait()
        for half in range(2):
            result[kept[half]] = joint[pl.ds(base + half * size, size)]

        for stage in reversed(range(len(bits))):
            size = trail[stage]
            copies = []
            for half in range(2):
                bit = orders[half][stage]
                here = pl.ds(pl.multiple_of(starts[half], 16), size)
                copies.append(
                    send(result.at[here], result.at[here], send_sem, recv_sem, index, partner[bit])
                )
                starts[half] = starts[half] - mine[bit] * size
                index += 1
            yield
            for copy in copies:
                copy.wait()
        for here, there, _, summed, lanes in segments(low, high):
            summed[there, lanes] = result[here].astype(jnp.float32)

    each = 4 * len(bits) + 2 * (slides - 1)
    running = [sum_rows(low, high, k * each) for k, (low, high) in enumerate(groups)]
    rounds = 0
    own_copies = []
    while running:
        left = []
        for group in running:
            try:
                next(group)
                left.append(group)
            except StopIteration:
                pass
        running = left
        if rounds == len(bits):
            own_copies = [
                send(own_ref, all_ref.at[me], own_send_sem, own_recv_sem, index, peer)
                for index, peer in enumerate(neighbours)
            ]
            all_ref[me] = own_ref[...]
        rounds += 1
    for copy in own_copies:
        copy.wait()


def sum_grads(g_w_in, g_w_out, others, own):
    strips, slides = lax.axis_size("strip"), lax.axis_size("slide")
    channels = g_w_out.shape[1]
    height, width = own.shape[:2]
    flat = [other.reshape(-1, channels) for other in others]
    unit = strips * slides * 16
    w_rows = g_w_in.size // channels + g_w_out.shape[0]
    used = w_rows + sum(other.shape[0] for other in flat)
    units = -(-used // unit)
    rows = units * unit
    if rows > used:
        flat.append(jnp.zeros((rows - used, channels), jnp.float32))
    rest = jnp.concatenate(flat, axis=0)
    parts = min(units, 3)
    edges = [-(-units * k // parts) * unit for k in range(parts + 1)]
    groups = tuple(zip(edges[:-1], edges[1:]))
    stages = strips.bit_length() - 1
    count = parts * (4 * stages + 2 * (slides - 1))
    piece = rows // strips
    small = jnp.bfloat16
    w_in_sum, w_out_sum, rest_sum, region = pl.pallas_call(
        functools.partial(sum_kernel, strips, slides, groups),
        out_shape=[
            jax.ShapeDtypeStruct(g_w_in.shape, jnp.float32),
            jax.ShapeDtypeStruct(g_w_out.shape, jnp.float32),
            jax.ShapeDtypeStruct(rest.shape, jnp.float32),
            jax.ShapeDtypeStruct((strips, height * width, channels), own.dtype),
        ],
        in_specs=[pl.BlockSpec(memory_space=pltpu.VMEM)] * 4,
        out_specs=[pl.BlockSpec(memory_space=pltpu.VMEM)] * 4,
        scratch_shapes=[
            pltpu.VMEM((rows, channels), jnp.float32),
            pltpu.VMEM((rows - piece, channels), small),
            pltpu.VMEM((rows - piece, channels), small),
            pltpu.VMEM((piece, channels), small),
            pltpu.VMEM(((slides - 1) * (piece // slides), channels), small),
            pltpu.VMEM((piece, channels), small),
            pltpu.VMEM((rows, channels), small),
            pltpu.SemaphoreType.DMA((count,)),
            pltpu.SemaphoreType.DMA((count,)),
            pltpu.SemaphoreType.DMA((strips - 1,)),
            pltpu.SemaphoreType.DMA((strips - 1,)),
        ],
        compiler_params=pltpu.CompilerParams(
            collective_id=3,
            has_side_effects=True,
            vmem_limit_bytes=vmem_for(
                ((3, rows, channels), 4),
                ((3, rows, channels), 2),
                ((3, piece, channels), 2),
                ((strips + 1, *own.shape), 2),
            ),
        ),
    )(g_w_in, g_w_out, rest, own.reshape(height * width, channels))
    summed, at = [], 0
    for other in others:
        length = other.size // channels
        summed.append(rest_sum[at : at + length].reshape(other.shape))
        at += length
    return w_in_sum, w_out_sum, summed, region.reshape(strips * height, width, channels)


def rows_around(region, margin, side, rows):
    padded = jnp.pad(region, ((margin, margin), (side, side), (0, 0)))
    start = lax.axis_index("strip") * rows
    return lax.dynamic_slice_in_dim(padded, start, rows + 2 * margin, axis=0)


def depth_conv(source, kernel, pad_rows, pad_cols):
    return lax.conv_general_dilated(
        source[None],
        kernel[:, :, None, :],
        (1, 1),
        ((pad_rows, pad_rows), (pad_cols, pad_cols)),
        dimension_numbers=("NHWC", "HWIO", "NHWC"),
        feature_group_count=source.shape[-1],
        preferred_element_type=jnp.float32,
    )[0]


def kernel_grad(padded, upstream):
    return lax.conv_general_dilated(
        padded[None],
        upstream[:, :, None, :],
        (1, 1),
        "VALID",
        dimension_numbers=("NHWC", "HWIO", "NHWC"),
        feature_group_count=padded.shape[-1],
        preferred_element_type=jnp.float32,
    )[0]


def local(
    image,
    cotangent,
    kernel_tall,
    kernel_wide,
    layer_norm_gain,
    layer_norm_bias,
    w_in,
    b_in,
    w_out,
    b_out,
):
    source = image[0]
    upstream = cotangent[0]
    row_count, full_width, channels = source.shape
    tall_pad = (kernel_tall.shape[0] - 1) // 2
    rim_width = (kernel_tall.shape[1] - 1) // 2
    wide_pad = (kernel_wide.shape[1] - 1) // 2
    scale_multiplier = jnp.float32(
        row_count * full_width * lax.axis_size("slide") * lax.axis_size("strip")
    ) ** (-0.5)
    reach = min(wide_pad, full_width - 1)
    near = kernel_wide[:, wide_pad - reach : wide_pad + reach + 1]
    region_rows = row_count * lax.axis_size("strip")
    window = rows_around(gather_rows(source, 0), tall_pad + rim_width, rim_width, row_count)
    place = (
        lax.axis_index("strip") * row_count
        - rim_width
        + lax.broadcasted_iota(jnp.int32, (row_count + 2 * rim_width, 1, 1), 0)
    )
    mixed_rows = jnp.where(
        (place >= 0) & (place < region_rows), depth_conv(window, kernel_tall, 0, 0), 0.0
    ).astype(jnp.bfloat16)
    conv_out = depth_conv(mixed_rows, near, 0, reach)
    mean_removed = conv_out - jnp.mean(conv_out, axis=-1, keepdims=True)
    inverse_deviation = lax.rsqrt(
        jnp.mean(mean_removed * mean_removed, axis=-1, keepdims=True) + epsilon
    )
    standardized_input = mean_removed * inverse_deviation
    normalized_output = (standardized_input * layer_norm_gain + layer_norm_bias).astype(
        jnp.bfloat16
    )
    flat_normed = normalized_output.reshape(-1, channels)
    pre_act = jnp.dot(flat_normed, w_in, preferred_element_type=jnp.float32) + b_in
    cdf_value = 0.5 * (1.0 + lax.erf(pre_act * 0.7071067811865476))
    hidden = (pre_act * cdf_value).astype(jnp.bfloat16)
    branch = jnp.dot(hidden, w_out, preferred_element_type=jnp.float32) + b_out
    output = (source.astype(jnp.float32) + branch.reshape(source.shape)).astype(jnp.bfloat16)
    flat_cot = upstream.reshape(-1, channels)
    g_w_out = jnp.dot(hidden.T, flat_cot, preferred_element_type=jnp.float32) * scale_multiplier
    g_b_out = jnp.sum(flat_cot.astype(jnp.float32), axis=0) * scale_multiplier
    d_hidden = jnp.dot(flat_cot, w_out.T, preferred_element_type=jnp.float32)
    slope = cdf_value + pre_act * jnp.exp(-0.5 * pre_act * pre_act) * 0.3989422804014327
    d_pre = (d_hidden * slope).astype(jnp.bfloat16)
    g_w_in = jnp.dot(flat_normed.T, d_pre, preferred_element_type=jnp.float32) * scale_multiplier
    g_b_in = jnp.sum(d_pre.astype(jnp.float32), axis=0) * scale_multiplier
    grad_layer_norm = jnp.dot(d_pre, w_in.T, preferred_element_type=jnp.float32).reshape(
        source.shape
    )
    grad_norm_gain = jnp.sum(grad_layer_norm * standardized_input, axis=(0, 1)) * scale_multiplier
    g_shift = jnp.sum(grad_layer_norm, axis=(0, 1)) * scale_multiplier
    grad_standardized = grad_layer_norm * layer_norm_gain
    grad_depth_output = (
        inverse_deviation
        * (
            grad_standardized
            - jnp.mean(grad_standardized, axis=-1, keepdims=True)
            - standardized_input
            * jnp.mean(grad_standardized * standardized_input, axis=-1, keepdims=True)
        )
    ).astype(jnp.bfloat16)
    d_conv_rims = add_rims(grad_depth_output, rim_width, 1)
    d_mixed = depth_conv(d_conv_rims, near[::-1, ::-1], 0, reach).astype(jnp.bfloat16)
    g_near = (
        kernel_grad(jnp.pad(mixed_rows, ((0, 0), (reach, reach), (0, 0))), grad_depth_output)
        * scale_multiplier
    )
    g_tall = (
        kernel_grad(
            jnp.swapaxes(window[rim_width:-rim_width], 0, 1), jnp.swapaxes(d_mixed, 0, 1)
        )
        * scale_multiplier
    )
    g_w_in, g_w_out, (g_tall, g_near, grad_norm_gain, g_shift, g_b_in, g_b_out), d_region = sum_grads(
        g_w_in,
        g_w_out,
        (g_tall, g_near, grad_norm_gain, g_shift, g_b_in, g_b_out),
        d_mixed,
    )
    d_mixed_window = rows_around(d_region, tall_pad, rim_width, row_count)
    d_image = depth_conv(d_mixed_window, kernel_tall[::-1, ::-1], 0, 0).astype(jnp.bfloat16)
    grad_image = (upstream.astype(jnp.float32) + d_image.astype(jnp.float32)).astype(jnp.bfloat16)
    g_wide = jnp.pad(g_near, ((0, 0), (wide_pad - reach, wide_pad - reach), (0, 0)))
    g_tall = jnp.swapaxes(g_tall, 0, 1)
    return (
        output[None],
        grad_image[None],
        g_tall,
        g_wide,
        grad_norm_gain,
        g_shift,
        g_w_in,
        g_b_in,
        g_w_out,
        g_b_out,
    )


def solution(mesh):
    placed = (
        P("slide", "strip", None, None),
        P("slide", "strip", None, None),
        P(),
        P(),
        P(),
        P(),
        P(),
        P(),
        P(),
        P(),
    )
    return jax.shard_map(
        local,
        mesh=mesh,
        in_specs=placed,
        out_specs=(
            P("slide", "strip", None, None),
            P("slide", "strip", None, None),
            P(),
            P(),
            P(),
            P(),
            P(),
            P(),
            P(),
            P(),
        ),
        check_vma=False,
    )
```
